32 devices in a mesh: groups: 2 (over y), tensor: 4 (over z), frames: 4 (over x, core).
Axes of the slice: x: 2, y: 2, z: 4, core: 2. Of those that a mesh axis runs over, the one named last changes fastest.
Arguments:
- patches: bfloat16 [256, 16, 3072], P('tensor', ('groups', 'frames')), parts along dimension 1, may hold values from -12 to 12
- ln_gain: float32 [3072], replicated, may hold values from 0.5 to 1.5
- in_weight: bfloat16 [3072, 4, 768], P('frames', 'tensor'), may hold values from -0.109375 to 0.109375
- q_gain: float32 [4, 128], P('tensor'), may hold values from 0.1 to 1.9
- k_gain: float32 [4, 128], P('tensor'), may hold values from 0.1 to 1.9
- out_weight: bfloat16 [4, 512, 3072], P('tensor', None, 'frames'), may hold values from -0.25 to 0.25
Outputs:
- encoded: bfloat16 [256, 16, 3072], P('tensor', ('groups', 'frames')), parts along dimension 1
The draws below stay inside these ranges and needn't reach their ends.
There are 2 independent parts, one for each index of `groups`. The reference program is written for one: setup_inputs(seed, part) draws one part's arguments, and reference() takes and returns one part's arrays. A program takes and returns all parts, laid end to end along the dimension named above; an argument that names none is the same for every part. Nothing has to cross between parts.
All inputs are finite; a program needn't handle non-finite values.
Results may differ from the reference program's by a relative error of at most 0.022.
Values may be sent and summed in bfloat16 or wider, within the bound.
A program may use at most 64 MiB of HBM per device.

```python
import math
import jax
import jax.numpy as jnp
from jax import lax

D = 3072
HD = 128
FF_BLOCK = 384
PATCHES = 256
HEADS = 4
FRAMES = 8


def draw_patches(key, part):
    base_key = jax.random.fold_in(key, 7)
    key_base, key_column, key_row = jax.random.split(base_key, 3)
    full_shape = (PATCHES, FRAMES, D)
    base_draw = jax.random.normal(key_base, full_shape, jnp.float32)
    column_scale = jnp.exp(jax.random.uniform(key_column, (D,), jnp.float32, math.log(0.4), math.log(2.5)))
    row_scale = jnp.exp(jax.random.uniform(key_row, (PATCHES, FRAMES, 1), jnp.float32, math.log(0.7), math.log(1.4)))
    return jnp.clip(base_draw * column_scale * row_scale, -12.0, 12.0).astype(jnp.bfloat16)


def steps_of(rng, extent, shards, low, largest):
    level = 1.0
    for position, shards_of in shards:
        draws = jax.random.uniform(jax.random.fold_in(jax.random.fold_in(rng, 6), position), (shards_of,), jnp.float32, low / len(shards), largest / len(shards))
        level = level * jnp.repeat(jnp.exp(draws), extent[position] // shards_of).reshape((-1,) + (1,) * (len(extent) - 1 - position))
    return level


def bell_draw(rng, shape, scale, limit, cuts=(), dtype=jnp.bfloat16):
    gain = steps_of(rng, shape, cuts, -0.22, 0.18) if cuts else 1.0
    values = jax.random.normal(rng, shape, jnp.float32) * scale * gain
    return jnp.minimum(jnp.maximum(values, -limit), limit).astype(dtype)


def setup_inputs(seed: int = 0, part: int = 0) -> dict:
    splits = jax.random.split(jax.random.key(seed), 7)
    part_splits = jax.random.split(jax.random.fold_in(splits[6], part), 7)
    return {
        "patches": draw_patches(jax.random.fold_in(jax.random.fold_in(splits[6], part), 71), part),
        "ln_gain": jnp.clip(1.0 + 0.1 * jax.random.normal(splits[1], (D,), jnp.float32), 0.5, 1.5),
        "in_weight": bell_draw(splits[2], (D, HEADS, 3 * HD + FF_BLOCK), D ** -0.5, 0.109375, ((0, 4), (1, 4))),
        "q_gain": jnp.clip(1.0 + 0.18 * jax.random.normal(splits[3], (HEADS, HD), jnp.float32), 0.1, 1.9),
        "k_gain": jnp.clip(1.0 + 0.18 * jax.random.normal(splits[4], (HEADS, HD), jnp.float32), 0.1, 1.9),
        "out_weight": bell_draw(splits[5], (HEADS, HD + FF_BLOCK, D), (HD + FF_BLOCK) ** -0.5, 0.25, ((0, 4), (2, 4))),
    }


def layer_norm(values, gain_vec):
    mean_val = lax.optimization_barrier(jnp.mean(values, axis=-1, keepdims=True))
    centered = values - mean_val
    variance = lax.optimization_barrier(jnp.mean(centered * centered, axis=-1, keepdims=True))
    return centered * lax.rsqrt(variance + 1e-06) * gain_vec

def reference(patches, ln_gain, in_weight, q_gain, k_gain, out_weight):
    normed = layer_norm(patches.astype(jnp.float32), ln_gain).astype(jnp.bfloat16)
    flat_rows = normed.reshape(PATCHES * FRAMES, D)
    logit_scale = 1.0 / math.sqrt(HD)

    def head_step(running, inputs):
        w_in, gain_q, gain_k, w_out = inputs
        joined_cols = jnp.dot(flat_rows, w_in, preferred_element_type=jnp.float32).reshape(PATCHES, FRAMES, 3 * HD + FF_BLOCK)
        query_slice = layer_norm(joined_cols[..., :HD], gain_q).astype(jnp.bfloat16)
        key_slice = layer_norm(joined_cols[..., HD:2 * HD], gain_k).astype(jnp.bfloat16)
        value_slice = joined_cols[..., 2 * HD:3 * HD].astype(jnp.bfloat16)
        hidden = jax.nn.gelu(joined_cols[..., 3 * HD:], approximate=False).astype(jnp.bfloat16)
        attention_logits = jnp.einsum('ldg,bdg->dlb', query_slice.astype(jnp.float32), key_slice.astype(jnp.float32)) * logit_scale
        exponent_scores = jnp.exp(attention_logits)
        softmax_total = lax.optimization_barrier(jnp.sum(exponent_scores, axis=-1))
        attention_output = jnp.einsum('jdl,ljg->djg', exponent_scores.astype(jnp.bfloat16).astype(jnp.float32), value_slice.astype(jnp.float32))
        attention_output = attention_output / jnp.transpose(softmax_total)[:, :, None]
        blended_rows = jnp.concatenate([attention_output.astype(jnp.bfloat16), hidden], axis=-1).reshape(PATCHES * FRAMES, HD + FF_BLOCK)
        partial_value = jnp.dot(blended_rows, w_out, preferred_element_type=jnp.float32).astype(jnp.bfloat16)
        partial_value = lax.optimization_barrier(partial_value)
        return (running + partial_value.astype(jnp.float32), None)
    in_heads = jnp.transpose(in_weight, (1, 0, 2))
    running, unused = lax.scan(head_step, jnp.zeros((PATCHES * FRAMES, D), jnp.float32), (in_heads, q_gain, k_gain, out_weight))
    return (patches.astype(jnp.float32) + running.reshape(PATCHES, FRAMES, D)).astype(jnp.bfloat16)
```

```python
import functools
import math

import jax
import jax.numpy as jnp
from jax import lax
from jax.experimental import pallas as pl
from jax.experimental.pallas import tpu as pltpu
from jax.sharding import PartitionSpec as P

MESH = pl.DeviceIdType.MESH


def norm(values, gain_vec):
    mean_val = jnp.mean(values, axis=-1, keepdims=True)
    centered = values - mean_val
    variance = jnp.mean(centered * centered, axis=-1, keepdims=True)
    return centered * lax.rsqrt(variance + 1e-06) * gain_vec


def kernel(ng, nt, nf, nlo, subs, x_ref, gain_ref, win_ref, qg_ref, kg_ref, wout_ref, out_ref,
           xg, w_in, w_out, joined, blended, part, rbuf,
           ag_send, ag_recv, rs_send, rs_recv, ws_send, ws_recv, own_sem):
    g, t, f = lax.axis_index("groups"), lax.axis_index("tensor"), lax.axis_index("frames")
    frames, rows, width = x_ref.shape
    head_dim = qg_ref.shape[1]
    nhi = nf // nlo
    hi, lo = f // nlo, f % nlo
    sibling = {"frames": hi * nlo + (nlo - 1 - lo)}
    right, left = {"tensor": lax.rem(t + 1, nt)}, {"tensor": lax.rem(t + nt - 1, nt)}

    barrier = pltpu.get_barrier_semaphore()

    def greet(device):
        pl.semaphore_signal(barrier, inc=1, device_id=device, device_id_type=MESH)

    pl.when(t + 1 < nt)(lambda: greet(right))
    pl.when(t > 0)(lambda: greet(left))
    if nlo > 1:
        greet(sibling)
    for j in range(1, nhi):
        greet({"frames": lax.rem(hi + j, nhi) * nlo + lo})
    for k in range(1, ng):
        greet({"groups": lax.rem(g + k, ng)})
    fixed = (nlo - 1) + (nhi - 1) + (ng - 1)
    pl.semaphore_wait(barrier, fixed + jnp.where(t + 1 < nt, 1, 0) + jnp.where(t > 0, 1, 0))

    held, given = (w_in, w_out), (win_ref, wout_ref)

    def piece(w, shard, section, sub):
        size = held[w].shape[1] // (ng * subs)
        start = pl.multiple_of((section * subs + sub) * size, size)
        return held[w].at[shard, pl.ds(start, size), :]

    def own_piece(w, section, sub):
        size = held[w].shape[1] // (ng * subs)
        start = pl.multiple_of((section * subs + sub) * size, size)
        return given[w].at[pl.ds(start, size), :]

    def move(w, shard, section, sub, slot, device, own=False):
        return pltpu.make_async_remote_copy(
            src_ref=own_piece(w, section, sub) if own else piece(w, shard, section, sub),
            dst_ref=piece(w, shard, section, sub),
            send_sem=ws_send.at[w, shard, section, sub, slot],
            recv_sem=ws_recv.at[w, shard, section, sub],
            device_id=device,
            device_id_type=MESH,
        )

    def w_own_across(w, act):
        for sub in range(subs):
            for j in range(1, nhi):
                act(move(w, f, g, sub, j - 1, {"frames": lax.rem(hi + j, nhi) * nlo + lo}, True))

    last = max(nhi - 1, ng - 1)

    def w_own_sibling(w, act):
        if nlo > 1:
            for section in range(ng):
                for sub in range(subs):
                    act(move(w, f, section, sub, last, sibling, True))

    def w_relay(w, sub, act, wait):
        for j in range(1, nhi):
            shard = lax.rem(hi + nhi - j, nhi) * nlo + lo
            if wait:
                move(w, shard, g, sub, 0, sibling).wait_recv()
            for k in range(1, ng):
                act(move(w, shard, g, sub, k - 1, {"groups": lax.rem(g + k, ng)}))
            if nlo > 1:
                act(move(w, shard, g, sub, last, sibling))

    def w_relay_two(w, sub, act, wait):
        for j in range(1, nhi):
            shard = lax.rem(hi + nhi - j, nhi) * nlo + lo
            for k in range(1, ng):
                section = lax.rem(g + k, ng)
                if wait:
                    move(w, shard, section, sub, 0, sibling).wait_recv()
                if nlo > 1:
                    act(move(w, shard, section, sub, last, sibling))

    def w_finish(w):
        if nlo > 1:
            for j in range(nhi):
                shard = j * nlo + (nlo - 1 - lo)
                for section in range(ng):
                    for sub in range(subs):
                        move(w, shard, section, sub, 0, sibling).wait_recv()
        pltpu.make_async_copy(given[w], held[w].at[f], own_sem.at[w]).wait()

    def start(copy):
        copy.start()

    def sent(copy):
        copy.wait_send()

    def w_sent(w):
        w_own_across(w, sent)
        w_own_sibling(w, sent)
        for sub in range(subs):
            w_relay(w, sub, sent, False)
            w_relay_two(w, sub, sent, False)

    def block(ref, fr, b):
        return ref.at[fr, pl.ds(pl.multiple_of(b * rows, rows), rows), :]

    def ag_copy(fr, b, way):
        return pltpu.make_async_remote_copy(
            src_ref=block(xg, fr, b),
            dst_ref=block(xg, fr, b),
            send_sem=ag_send.at[fr, way, b],
            recv_sem=ag_recv.at[fr, b],
            device_id=right if way == 0 else left,
            device_id_type=MESH,
        )

    def ag_own(fr, act):
        pl.when(t + 1 < nt)(lambda: act(ag_copy(fr, t, 0)))
        pl.when(t > 0)(lambda: act(ag_copy(fr, t, 1)))

    def ag_step(fr, s, act, wait):
        b = t - 1 - s

        @pl.when(b >= 0)
        def _():
            if wait:
                ag_copy(fr, b, 0).wait_recv()
            pl.when(t + 1 < nt)(lambda: act(ag_copy(fr, b, 0)))

        c = t + 1 + s

        @pl.when(c < nt)
        def _():
            if wait:
                ag_copy(fr, c, 1).wait_recv()
            pl.when(t > 0)(lambda: act(ag_copy(fr, c, 1)))

    def rs_copy(fr, d, way, first):
        slot = d if way == 0 else jnp.where(d == t - 1, nt, d)
        return pltpu.make_async_remote_copy(
            src_ref=block(part, fr, d) if first else rbuf.at[fr, d],
            dst_ref=rbuf.at[fr, slot],
            send_sem=rs_send.at[fr, d],
            recv_sem=rs_recv.at[fr, slot],
            device_id=right if way == 0 else left,
            device_id_type=MESH,
        )

    def rs_arrived(fr, slot):
        pltpu.make_async_remote_copy(
            src_ref=rbuf.at[fr, slot],
            dst_ref=rbuf.at[fr, slot],
            send_sem=rs_send.at[fr, 0],
            recv_sem=rs_recv.at[fr, slot],
            device_id=right,
            device_id_type=MESH,
        ).wait_recv()

    def rs_send_on(fr, d, way, edge):
        @pl.when(edge)
        def _():
            rs_copy(fr, d, way, True).start()

        @pl.when(jnp.logical_not(edge))
        def _():
            rs_arrived(fr, d)
            mine = block(part, fr, d)[...].astype(jnp.float32)
            rbuf[fr, d] = (rbuf[fr, d].astype(jnp.float32) + mine).astype(jnp.bfloat16)
            rs_copy(fr, d, way, False).start()

    def rs_step(fr, s):
        d = nt - 1 - s
        pl.when(d > t)(lambda: rs_send_on(fr, d, 0, t == 0))
        pl.when(s < t)(lambda: rs_send_on(fr, s, 1, t == nt - 1))

    def rs_sent(fr):
        for d in range(nt):
            @pl.when(d != t)
            def _():
                rs_copy(fr, d, 0, True).wait_send()

    def rs_finish(fr):
        out_ref[fr] = (x_ref[fr].astype(jnp.float32) + block(part, fr, t)[...].astype(jnp.float32)).astype(jnp.float32)

        @pl.when(t > 0)
        def _():
            rs_arrived(fr, t)
            out_ref[fr] += rbuf[fr, t].astype(jnp.float32)

        @pl.when(t + 1 < nt)
        def _():
            rs_arrived(fr, nt)
            out_ref[fr] += rbuf[fr, nt].astype(jnp.float32)

    def normalise(fr):
        values = norm(x_ref[fr].astype(jnp.float32), gain_ref[...]).astype(jnp.bfloat16)
        block(xg, fr, t)[...] = values

    def project(fr):
        tile = 256 if joined.shape[1] % 256 == 0 else joined.shape[1]

        @pl.loop(0, joined.shape[1] // tile)
        def _(n):
            cols = pl.ds(pl.multiple_of(n * tile, tile), tile)
            weight = w_in[:, :, cols].reshape(width, tile)
            joined[:, cols] = jnp.dot(xg[fr], weight, preferred_element_type=jnp.float32)

        query = norm(joined[:, :head_dim], qg_ref[...]).astype(jnp.bfloat16)
        key = norm(joined[:, head_dim:2 * head_dim], kg_ref[...]).astype(jnp.bfloat16)
        value = joined[:, 2 * head_dim:3 * head_dim].astype(jnp.bfloat16)
        raw = joined[:, 3 * head_dim:]
        blended[:, head_dim:] = (0.5 * raw * (1.0 + lax.erf(raw * math.sqrt(0.5)))).astype(jnp.bfloat16)
        scores = lax.dot_general(query, key, (((1,), (1,)), ((), ())), preferred_element_type=jnp.float32)
        exp_scores = jnp.exp(scores * (1.0 / math.sqrt(head_dim)))
        total = jnp.sum(exp_scores, axis=-1, keepdims=True)
        attended = jnp.dot(exp_scores.astype(jnp.bfloat16), value, preferred_element_type=jnp.float32)
        blended[:, :head_dim] = (attended / total).astype(jnp.bfloat16)

    def contribute(fr):
        cols = w_out.shape[2]

        @pl.loop(0, nf)
        def _(n):
            part[fr, :, pl.ds(pl.multiple_of(n * cols, cols), cols)] = jnp.dot(
                blended[...], w_out[n], preferred_element_type=jnp.float32
            ).astype(jnp.bfloat16)

    for w in range(2):
        pltpu.make_async_copy(given[w], held[w].at[f], own_sem.at[w]).start()
    w_own_across(0, start)
    w_own_sibling(0, start)
    normalise(0)
    ag_own(0, start)
    for fr in range(1, frames):
        normalise(fr)

    tasks = [functools.partial(w_relay, 0, sub, start, True) for sub in range(subs)]
    tasks += [functools.partial(w_own_across, 1, start), functools.partial(w_own_sibling, 1, start)]
    tasks += [functools.partial(w_relay_two, 0, sub, start, True) for sub in range(subs)]
    tasks += [functools.partial(w_relay, 1, sub, start, True) for sub in range(subs)]
    done = 0
    for s in range(nt - 1):
        until = -(-len(tasks) * (s + 1) // (nt - 1))
        for task in tasks[done:until]:
            task()
        done = until
        ag_step(0, s, start, True)
    for fr in range(frames):
        if fr + 1 < frames:
            ag_own(fr + 1, start)
        if fr == 0:
            w_finish(0)
        project(fr)
        if fr == 0:
            for sub in range(subs):
                w_relay_two(1, sub, start, True)
            w_finish(1)
        contribute(fr)
        for s in range(nt - 1):
            if fr + 1 < frames:
                ag_step(fr + 1, s, start, True)
            rs_step(fr, s)
    for fr in range(frames):
        rs_finish(fr)

    for w in range(2):
        w_sent(w)
    for fr in range(frames):
        ag_own(fr, sent)
        for s in range(nt - 1):
            ag_step(fr, s, sent, False)
        rs_sent(fr)


def local(ng, nt, nf, patches, ln_gain, in_weight, q_gain, k_gain, out_weight):
    rows, frames, width = patches.shape
    depth, _, joined_cols = in_weight.shape
    _, out_rows, out_cols = out_weight.shape
    nlo = 2 if nf % 2 == 0 else 1
    nhi = nf // nlo
    subs = 2 if depth % (ng * 32) == 0 and out_rows % (ng * 32) == 0 else 1
    slots = max(nhi - 1, ng - 1) + 1
    everyone = nt * rows
    vmem = pl.BlockSpec(memory_space=pltpu.VMEM)
    hbm = pl.BlockSpec(memory_space=pl.ANY)
    bf16, f32 = jnp.bfloat16, jnp.float32
    dma = pltpu.SemaphoreType.DMA
    summed = pl.pallas_call(
        functools.partial(kernel, ng, nt, nf, nlo, subs),
        out_shape=jax.ShapeDtypeStruct((frames, rows, width), f32),
        in_specs=[vmem, vmem, hbm, vmem, vmem, hbm],
        out_specs=vmem,
        scratch_shapes=[
            pltpu.VMEM((frames, everyone, width), bf16),
            pltpu.VMEM((nf, depth, joined_cols), bf16),
            pltpu.VMEM((nf, out_rows, out_cols), bf16),
            pltpu.VMEM((everyone, joined_cols), f32),
            pltpu.VMEM((everyone, out_rows), bf16),
            pltpu.VMEM((frames, everyone, width), bf16),
            pltpu.VMEM((frames, nt + 1, rows, width), bf16),
            dma((frames, 2, nt)),
            dma((frames, nt)),
            dma((frames, nt)),
            dma((frames, nt + 1)),
            dma((2, nf, ng, subs, slots)),
            dma((2, nf, ng, subs)),
            dma((2,)),
        ],
        compiler_params=pltpu.CompilerParams(
            collective_id=0, has_side_effects=True, vmem_limit_bytes=48 * 1024 * 1024
        ),
    )(
        jnp.transpose(patches, (1, 0, 2)),
        ln_gain.reshape(1, width),
        in_weight.reshape(depth, joined_cols),
        q_gain,
        k_gain,
        out_weight.reshape(out_rows, out_cols),
    )
    return jnp.transpose(summed, (1, 0, 2)).astype(jnp.bfloat16)


def solution(mesh):
    sizes = [mesh.shape[name] for name in ("groups", "tensor", "frames")]
    return jax.shard_map(
        functools.partial(local, *sizes),
        mesh=mesh,
        in_specs=(
            P("tensor", ("groups", "frames"), None),
            P(),
            P("frames", "tensor", None),
            P("tensor", None),
            P("tensor", None),
            P("tensor", None, "frames"),
        ),
        out_specs=P("tensor", ("groups", "frames"), None),
        check_vma=False,
    )
```

```python
import functools
import math

import jax
import jax.numpy as jnp
from jax import lax
from jax.experimental import pallas as pl
from jax.experimental.pallas import tpu as pltpu
from jax.sharding import PartitionSpec as P

MESH = pl.DeviceIdType.MESH


def norm(values, gain_vec):
    mean_val = jnp.mean(values, axis=-1, keepdims=True)
    centered = values - mean_val
    variance = jnp.mean(centered * centered, axis=-1, keepdims=True)
    return centered * lax.rsqrt(variance + 1e-06) * gain_vec


def kernel(ng, nt, nf, nlo, subs, x_ref, gain_ref, win_ref, qg_ref, kg_ref, wout_ref, out_ref,
           xg, w_in, w_out, joined, qkv, blended, part, rbuf,
           ag_send, ag_recv, rs_send, rs_recv, ws_send, ws_recv, own_sem):
    g, t, f = lax.axis_index("groups"), lax.axis_index("tensor"), lax.axis_index("frames")
    frames, rows, width = x_ref.shape
    head_dim = qg_ref.shape[1]
    nhi = nf // nlo
    hi, lo = f // nlo, f % nlo
    sibling = {"frames": hi * nlo + (nlo - 1 - lo)}
    right, left = {"tensor": lax.rem(t + 1, nt)}, {"tensor": lax.rem(t + nt - 1, nt)}

    barrier = pltpu.get_barrier_semaphore()

    def greet(device):
        pl.semaphore_signal(barrier, inc=1, device_id=device, device_id_type=MESH)

    pl.when(t + 1 < nt)(lambda: greet(right))
    pl.when(t > 0)(lambda: greet(left))
    if nlo > 1:
        greet(sibling)
    for j in range(1, nhi):
        greet({"frames": lax.rem(hi + j, nhi) * nlo + lo})
    for k in range(1, ng):
        greet({"groups": lax.rem(g + k, ng)})
    fixed = (nlo - 1) + (nhi - 1) + (ng - 1)
    pl.semaphore_wait(barrier, fixed + jnp.where(t + 1 < nt, 1, 0) + jnp.where(t > 0, 1, 0))

    held, given = (w_in, w_out), (win_ref, wout_ref)

    def piece(w, shard, section, sub):
        size = held[w].shape[1] // (ng * subs)
        start = pl.multiple_of((section * subs + sub) * size, size)
        return held[w].at[shard, pl.ds(start, size), :]

    def own_piece(w, section, sub):
        size = held[w].shape[1] // (ng * subs)
        start = pl.multiple_of((section * subs + sub) * size, size)
        return given[w].at[pl.ds(start, size), :]

    def move(w, shard, section, sub, slot, device, own=False):
        return pltpu.make_async_remote_copy(
            src_ref=own_piece(w, section, sub) if own else piece(w, shard, section, sub),
            dst_ref=piece(w, shard, section, sub),
            send_sem=ws_send.at[w, shard, section, sub, slot],
            recv_sem=ws_recv.at[w, shard, section, sub],
            device_id=device,
            device_id_type=MESH,
        )

    def w_own_across(w, act):
        for sub in range(subs):
            for j in range(1, nhi):
                act(move(w, f, g, sub, j - 1, {"frames": lax.rem(hi + j, nhi) * nlo + lo}, True))

    last = max(nhi - 1, ng - 1)

    def w_own_sibling(w, act):
        if nlo > 1:
            for section in range(ng):
                for sub in range(subs):
                    act(move(w, f, section, sub, last, sibling, True))

    def w_relay(w, sub, act, wait):
        for j in range(1, nhi):
            shard = lax.rem(hi + nhi - j, nhi) * nlo + lo
            if wait:
                move(w, shard, g, sub, 0, sibling).wait_recv()
            for k in range(1, ng):
                act(move(w, shard, g, sub, k - 1, {"groups": lax.rem(g + k, ng)}))
            if nlo > 1:
                act(move(w, shard, g, sub, last, sibling))

    def w_relay_two(w, sub, act, wait):
        for j in range(1, nhi):
            shard = lax.rem(hi + nhi - j, nhi) * nlo + lo
            for k in range(1, ng):
                section = lax.rem(g + k, ng)
                if wait:
                    move(w, shard, section, sub, 0, sibling).wait_recv()
                if nlo > 1:
                    act(move(w, shard, section, sub, last, sibling))

    def w_finish(w):
        if nlo > 1:
            for j in range(nhi):
                shard = j * nlo + (nlo - 1 - lo)
                for section in range(ng):
                    for sub in range(subs):
                        move(w, shard, section, sub, 0, sibling).wait_recv()
        pltpu.make_async_copy(given[w], held[w].at[f], own_sem.at[w]).wait()

    def start(copy):
        copy.start()

    def sent(copy):
        copy.wait_send()

    def w_sent(w):
        w_own_across(w, sent)
        w_own_sibling(w, sent)
        for sub in range(subs):
            w_relay(w, sub, sent, False)
            w_relay_two(w, sub, sent, False)

    def block(ref, fr, b):
        return ref.at[fr, pl.ds(pl.multiple_of(b * rows, rows), rows), :]

    def ag_copy(fr, b, way):
        return pltpu.make_async_remote_copy(
            src_ref=block(xg, fr, b),
            dst_ref=block(xg, fr, b),
            send_sem=ag_send.at[fr, way, b],
            recv_sem=ag_recv.at[fr, b],
            device_id=right if way == 0 else left,
            device_id_type=MESH,
        )

    def ag_own(fr, act):
        pl.when(t + 1 < nt)(lambda: act(ag_copy(fr, t, 0)))
        pl.when(t > 0)(lambda: act(ag_copy(fr, t, 1)))

    def ag_tick(k, act, wait):
        for way, count, can_send in ((0, t, t + 1 < nt), (1, nt - 1 - t, t > 0)):
            @pl.when(k < frames * count)
            def _(way=way, count=count, can_send=can_send):
                fr, i = k // jnp.maximum(count, 1), k % jnp.maximum(count, 1)
                b = t - 1 - i if way == 0 else t + 1 + i
                if wait:
                    ag_copy(fr, b, way).wait_recv()

                @pl.when(can_send)
                def _():
                    act(ag_copy(fr, b, way))
                    pl.when((i == count - 1) & (fr + 1 < frames))(lambda: act(ag_copy(fr + 1, t, way)))

            pl.when((k + 1 < frames) & (count == 0) & can_send)(lambda way=way: act(ag_copy(k + 1, t, way)))

    def rs_copy(fr, d, way, first):
        slot = d if way == 0 else jnp.where(d == t - 1, nt, d)
        return pltpu.make_async_remote_copy(
            src_ref=block(part, fr, d) if first else rbuf.at[fr, d],
            dst_ref=rbuf.at[fr, slot],
            send_sem=rs_send.at[fr, d],
            recv_sem=rs_recv.at[fr, slot],
            device_id=right if way == 0 else left,
            device_id_type=MESH,
        )

    def rs_arrived(fr, slot):
        pltpu.make_async_remote_copy(
            src_ref=rbuf.at[fr, slot],
            dst_ref=rbuf.at[fr, slot],
            send_sem=rs_send.at[fr, 0],
            recv_sem=rs_recv.at[fr, slot],
            device_id=right,
            device_id_type=MESH,
        ).wait_recv()

    def rs_edge(fr):
        for way, here, order in ((0, t == 0, range(nt - 1, 0, -1)), (1, t == nt - 1, range(nt - 1))):
            @pl.when(here)
            def _(way=way, order=order):
                for d in order:
                    rs_copy(fr, d, way, True).start()

    def rs_step(fr, s):
        for way, d, here in ((0, nt - 1 - s, (nt - 1 - s > t) & (t > 0)), (1, s, (s < t) & (t < nt - 1))):
            @pl.when(here)
            def _(way=way, d=d):
                rs_arrived(fr, d)
                mine = block(part, fr, d)[...].astype(jnp.float32)
                rbuf[fr, d] = (rbuf[fr, d].astype(jnp.float32) + mine).astype(jnp.bfloat16)
                rs_copy(fr, d, way, False).start()

    def rs_sent(fr):
        for d in range(nt):
            pl.when(d != t)(lambda d=d: rs_copy(fr, d, 0, True).wait_send())

    def rs_finish(fr):
        out_ref[fr] = (x_ref[fr].astype(jnp.float32) + block(part, fr, t)[...].astype(jnp.float32)).astype(jnp.float32)

        @pl.when(t > 0)
        def _():
            rs_arrived(fr, t)
            out_ref[fr] += rbuf[fr, t].astype(jnp.float32)

        @pl.when(t + 1 < nt)
        def _():
            rs_arrived(fr, nt)
            out_ref[fr] += rbuf[fr, nt].astype(jnp.float32)

    def normalise(fr):
        values = norm(x_ref[fr].astype(jnp.float32), gain_ref[...]).astype(jnp.bfloat16)
        block(xg, fr, t)[...] = values

    def project(fr, b):
        at = pl.ds(pl.multiple_of(b * rows, rows), rows)
        tile = 256 if joined.shape[1] % 256 == 0 else joined.shape[1]
        for n in range(joined.shape[1] // tile):
            cols = pl.ds(n * tile, tile)
            weight = w_in[:, :, cols].reshape(width, tile)
            joined[:, cols] = jnp.dot(xg[fr, at, :], weight, preferred_element_type=jnp.float32)
        bf16 = jnp.bfloat16
        qkv[at, :head_dim] = norm(joined[:, :head_dim], qg_ref[...]).astype(bf16)
        qkv[at, head_dim:2 * head_dim] = norm(joined[:, head_dim:2 * head_dim], kg_ref[...]).astype(bf16)
        qkv[at, 2 * head_dim:] = joined[:, 2 * head_dim:3 * head_dim].astype(bf16)
        raw = joined[:, 3 * head_dim:]
        blended[at, head_dim:] = (0.5 * raw * (1.0 + lax.erf(raw * math.sqrt(0.5)))).astype(bf16)

    def project_step(fr, s):
        pl.when(t - 1 - s >= 0)(lambda: project(fr, t - 1 - s))
        pl.when(t + 1 + s < nt)(lambda: project(fr, t + 1 + s))

    def attend():
        query, key, value = (qkv[:, i * head_dim:(i + 1) * head_dim] for i in range(3))
        scores = lax.dot_general(query, key, (((1,), (1,)), ((), ())), preferred_element_type=jnp.float32)
        exp_scores = jnp.exp(scores * (1.0 / math.sqrt(head_dim)))
        total = jnp.sum(exp_scores, axis=-1, keepdims=True)
        attended = jnp.dot(exp_scores.astype(jnp.bfloat16), value, preferred_element_type=jnp.float32)
        blended[:, :head_dim] = (attended / total).astype(jnp.bfloat16)

    def contribute(fr):
        cols = w_out.shape[2]

        @pl.loop(0, nf)
        def _(n):
            part[fr, :, pl.ds(pl.multiple_of(n * cols, cols), cols)] = jnp.dot(
                blended[...], w_out[n], preferred_element_type=jnp.float32
            ).astype(jnp.bfloat16)

    for w in range(2):
        pltpu.make_async_copy(given[w], held[w].at[f], own_sem.at[w]).start()
    w_own_across(0, start)
    normalise(0)
    ag_own(0, start)
    w_own_sibling(0, start)
    w_own_across(1, start)
    for fr in range(1, frames):
        normalise(fr)
    w_own_sibling(1, start)

    def relays(step, w, lowest, highest):
        return [functools.partial(step, w, sub, start, True) for sub in range(lowest, min(highest, subs))]

    groups = [
        relays(w_relay, 0, 0, 1),
        relays(w_relay, 0, 1, subs) + relays(w_relay_two, 0, 0, 1) + relays(w_relay, 1, 0, 1),
        relays(w_relay_two, 0, 1, subs) + relays(w_relay, 1, 1, subs) + relays(w_relay_two, 1, 0, subs - 1),
    ]
    for k in range(nt - 2):
        for task in groups.pop(0) if groups else ():
            task()
        ag_tick(k, start, True)
    for task in sum(groups, []):
        task()
    w_finish(0)
    project(0, t)
    pl.loop(0, nt - 2)(lambda s: project_step(0, s))
    ag_tick(nt - 2, start, True)
    project_step(0, nt - 2)
    for task in relays(w_relay_two, 1, subs - 1, subs):
        task()
    attend()
    w_finish(1)
    for fr in range(frames):
        contribute(fr)
        rs_edge(fr)
        if fr + 1 < frames:
            project(fr + 1, t)

        @pl.loop(0, nt - 1)
        def _(s, fr=fr):
            if fr + 1 < frames:
                ag_tick((fr + 1) * (nt - 1) + s, start, True)
            rs_step(fr, s)
            if fr + 1 < frames:
                project_step(fr + 1, s)

        if fr + 1 < frames:
            attend()
    for fr in range(frames):
        rs_finish(fr)

    for w in range(2):
        w_sent(w)
    for fr in range(frames):
        rs_sent(fr)
    ag_own(0, sent)
    for k in range(frames * (nt - 1)):
        ag_tick(k, sent, False)


def local(ng, nt, nf, patches, ln_gain, in_weight, q_gain, k_gain, out_weight):
    rows, frames, width = patches.shape
    depth, _, joined_cols = in_weight.shape
    _, out_rows, out_cols = out_weight.shape
    nlo = 2 if nf % 2 == 0 else 1
    nhi = nf // nlo
    subs = 2 if depth % (ng * 32) == 0 and out_rows % (ng * 32) == 0 else 1
    slots = max(nhi - 1, ng - 1) + 1
    everyone = nt * rows
    vmem = pl.BlockSpec(memory_space=pltpu.VMEM)
    hbm = pl.BlockSpec(memory_space=pl.ANY)
    bf16, f32 = jnp.bfloat16, jnp.float32
    dma = pltpu.SemaphoreType.DMA
    summed = pl.pallas_call(
        functools.partial(kernel, ng, nt, nf, nlo, subs),
        out_shape=jax.ShapeDtypeStruct((frames, rows, width), f32),
        in_specs=[vmem, vmem, hbm, vmem, vmem, hbm],
        out_specs=vmem,
        scratch_shapes=[
            pltpu.VMEM((frames, everyone, width), bf16),
            pltpu.VMEM((nf, depth, joined_cols), bf16),
            pltpu.VMEM((nf, out_rows, out_cols), bf16),
            pltpu.VMEM((rows, joined_cols), f32),
            pltpu.VMEM((everyone, 3 * q_gain.shape[1]), bf16),
            pltpu.VMEM((everyone, out_rows), bf16),
            pltpu.VMEM((frames, everyone, width), bf16),
            pltpu.VMEM((frames, nt + 1, rows, width), bf16),
            dma((frames, 2, nt)),
            dma((frames, nt)),
            dma((frames, nt)),
            dma((frames, nt + 1)),
            dma((2, nf, ng, subs, slots)),
            dma((2, nf, ng, subs)),
            dma((2,)),
        ],
        compiler_params=pltpu.CompilerParams(
            collective_id=0, has_side_effects=True, vmem_limit_bytes=48 * 1024 * 1024
        ),
    )(
        jnp.transpose(patches, (1, 0, 2)),
        ln_gain.reshape(1, width),
        in_weight.reshape(depth, joined_cols),
        q_gain,
        k_gain,
        out_weight.reshape(out_rows, out_cols),
    )
    return jnp.transpose(summed, (1, 0, 2)).astype(jnp.bfloat16)


def solution(mesh):
    sizes = [mesh.shape[name] for name in ("groups", "tensor", "frames")]
    return jax.shard_map(
        functools.partial(local, *sizes),
        mesh=mesh,
        in_specs=(
            P("tensor", ("groups", "frames"), None),
            P(),
            P("frames", "tensor", None),
            P("tensor", None),
            P("tensor", None),
            P("tensor", None, "frames"),
        ),
        out_specs=P("tensor", ("groups", "frames"), None),
        check_vma=False,
    )
```

```python
import functools
import math

import jax
import jax.numpy as jnp
from jax import lax
from jax.experimental import pallas as pl
from jax.experimental.pallas import tpu as pltpu
from jax.sharding import PartitionSpec as P

MESH = pl.DeviceIdType.MESH


def norm(values, gain_vec):
    mean_val = jnp.mean(values, axis=-1, keepdims=True)
    centered = values - mean_val
    variance = jnp.mean(centered * centered, axis=-1, keepdims=True)
    return centered * lax.rsqrt(variance + 1e-06) * gain_vec


def kernel(ng, nt, nf, nlo, subs, x_ref, gain_ref, win_ref, qg_ref, kg_ref, wout_ref, out_ref,
           xg, w_in, w_out, joined, qkv, blended, part, rbuf,
           ag_send, ag_recv, rs_send, rs_recv, ws_send, ws_recv, own_sem):
    g, t, f = lax.axis_index("groups"), lax.axis_index("tensor"), lax.axis_index("frames")
    frames, rows, width = x_ref.shape
    head_dim = qg_ref.shape[1]
    nhi = nf // nlo
    hi, lo = f // nlo, f % nlo
    sibling = {"frames": hi * nlo + (nlo - 1 - lo)}
    right, left = {"tensor": lax.rem(t + 1, nt)}, {"tensor": lax.rem(t + nt - 1, nt)}

    barrier = pltpu.get_barrier_semaphore()

    def greet(device):
        pl.semaphore_signal(barrier, inc=1, device_id=device, device_id_type=MESH)

    pl.when(t + 1 < nt)(lambda: greet(right))
    pl.when(t > 0)(lambda: greet(left))
    if nlo > 1:
        greet(sibling)
    for j in range(1, nhi):
        greet({"frames": lax.rem(hi + j, nhi) * nlo + lo})
    for k in range(1, ng):
        greet({"groups": lax.rem(g + k, ng)})
    fixed = (nlo - 1) + (nhi - 1) + (ng - 1)
    pl.semaphore_wait(barrier, fixed + jnp.where(t + 1 < nt, 1, 0) + jnp.where(t > 0, 1, 0))

    held, given = (w_in, w_out), (win_ref, wout_ref)

    def piece(w, shard, section, sub):
        size = held[w].shape[1] // (ng * subs)
        start = pl.multiple_of((section * subs + sub) * size, size)
        return held[w].at[shard, pl.ds(start, size), :]

    def own_piece(w, section, sub):
        size = held[w].shape[1] // (ng * subs)
        start = pl.multiple_of((section * subs + sub) * size, size)
        return given[w].at[pl.ds(start, size), :]

    def move(w, shard, section, sub, slot, device, own=False):
        return pltpu.make_async_remote_copy(
            src_ref=own_piece(w, section, sub) if own else piece(w, shard, section, sub),
            dst_ref=piece(w, shard, section, sub),
            send_sem=ws_send.at[w, shard, section, sub, slot],
            recv_sem=ws_recv.at[w, shard, section, sub],
            device_id=device,
            device_id_type=MESH,
        )

    def w_own_across(w, act):
        for sub in range(subs):
            for j in range(1, nhi):
                act(move(w, f, g, sub, j - 1, {"frames": lax.rem(hi + j, nhi) * nlo + lo}, True))

    last = max(nhi - 1, ng - 1)

    def w_own_sibling(w, act):
        if nlo > 1:
            for section in range(ng):
                for sub in range(subs):
                    act(move(w, f, section, sub, last, sibling, True))

    def w_relay(w, sub, act, wait):
        for j in range(1, nhi):
            shard = lax.rem(hi + nhi - j, nhi) * nlo + lo
            if wait:
                move(w, shard, g, sub, 0, sibling).wait_recv()
            for k in range(1, ng):
                act(move(w, shard, g, sub, k - 1, {"groups": lax.rem(g + k, ng)}))
            if nlo > 1:
                act(move(w, shard, g, sub, last, sibling))

    def w_relay_two(w, sub, act, wait):
        for j in range(1, nhi):
            shard = lax.rem(hi + nhi - j, nhi) * nlo + lo
            for k in range(1, ng):
                section = lax.rem(g + k, ng)
                if wait:
                    move(w, shard, section, sub, 0, sibling).wait_recv()
                if nlo > 1:
                    act(move(w, shard, section, sub, last, sibling))

    def w_ready(w, j):
        pair = lax.rem(hi + j, nhi)
        if nlo > 1:
            for section in range(ng):
                for sub in range(subs):
                    move(w, pair * nlo + (nlo - 1 - lo), section, sub, 0, sibling).wait_recv()
        if j == 0:
            pltpu.make_async_copy(given[w], held[w].at[f], own_sem.at[w]).wait()

    def start(copy):
        copy.start()

    def sent(copy):
        copy.wait_send()

    def w_sent(w):
        w_own_across(w, sent)
        w_own_sibling(w, sent)
        for sub in range(subs):
            w_relay(w, sub, sent, False)
            w_relay_two(w, sub, sent, False)

    def block(ref, fr, b):
        return ref.at[fr, pl.ds(pl.multiple_of(b * rows, rows), rows), :]

    def ag_copy(fr, b, way):
        return pltpu.make_async_remote_copy(
            src_ref=block(xg, fr, b),
            dst_ref=block(xg, fr, b),
            send_sem=ag_send.at[fr, way, b],
            recv_sem=ag_recv.at[fr, b],
            device_id=right if way == 0 else left,
            device_id_type=MESH,
        )

    def ag_own(fr, act):
        pl.when(t + 1 < nt)(lambda: act(ag_copy(fr, t, 0)))
        pl.when(t > 0)(lambda: act(ag_copy(fr, t, 1)))

    def ag_tick(k, act, wait):
        for way, count, can_send in ((0, t, t + 1 < nt), (1, nt - 1 - t, t > 0)):
            @pl.when(k < frames * count)
            def _(way=way, count=count, can_send=can_send):
                fr, i = k // jnp.maximum(count, 1), k % jnp.maximum(count, 1)
                b = t - 1 - i if way == 0 else t + 1 + i
                if wait:
                    ag_copy(fr, b, way).wait_recv()

                @pl.when(can_send)
                def _():
                    act(ag_copy(fr, b, way))
                    pl.when((i == count - 1) & (fr + 1 < frames))(lambda: act(ag_copy(fr + 1, t, way)))

            pl.when((k + 1 < frames) & (count == 0) & can_send)(lambda way=way: act(ag_copy(k + 1, t, way)))

    def sums(fr, c, d):
        return part.at[fr, c, pl.ds(pl.multiple_of(d * rows, rows), rows), :]

    def rs_copy(fr, c, d, way, first):
        slot = d if way == 0 else jnp.where(d == t - 1, nt, d)
        return pltpu.make_async_remote_copy(
            src_ref=sums(fr, c, d) if first else rbuf.at[fr, c, d],
            dst_ref=rbuf.at[fr, c, slot],
            send_sem=rs_send.at[fr, c, d],
            recv_sem=rs_recv.at[fr, c, slot],
            device_id=right if way == 0 else left,
            device_id_type=MESH,
        )

    def rs_arrived(fr, c, slot):
        pltpu.make_async_remote_copy(
            src_ref=rbuf.at[fr, c, slot],
            dst_ref=rbuf.at[fr, c, slot],
            send_sem=rs_send.at[fr, c, 0],
            recv_sem=rs_recv.at[fr, c, slot],
            device_id=right,
            device_id_type=MESH,
        ).wait_recv()

    def rs_edge(fr, c):
        for way, here, order in ((0, t == 0, range(nt - 1, 0, -1)), (1, t == nt - 1, range(nt - 1))):
            @pl.when(here)
            def _(way=way, order=order):
                for d in order:
                    rs_copy(fr, c, d, way, True).start()

    def rs_step(fr, c, s):
        for way, d, here in ((0, nt - 1 - s, (nt - 1 - s > t) & (t > 0)), (1, s, (s < t) & (t < nt - 1))):
            @pl.when(here)
            def _(way=way, d=d):
                rs_arrived(fr, c, d)
                mine = sums(fr, c, d)[...].astype(jnp.float32)
                rbuf[fr, c, d] = (rbuf[fr, c, d].astype(jnp.float32) + mine).astype(jnp.bfloat16)
                rs_copy(fr, c, d, way, False).start()

    def rs_sent(fr, c):
        for d in range(nt):
            pl.when(d != t)(lambda d=d: rs_copy(fr, c, d, 0, True).wait_send())

    def rs_finish(fr, c):
        size = width // nhi
        cols = pl.ds(pl.multiple_of(c * size, size), size)
        out_ref[fr, :, cols] = x_ref[fr, :, cols].astype(jnp.float32) + sums(fr, c, t)[...].astype(jnp.float32)

        @pl.when(t > 0)
        def _():
            rs_arrived(fr, c, t)
            out_ref[fr, :, cols] += rbuf[fr, c, t].astype(jnp.float32)

        @pl.when(t + 1 < nt)
        def _():
            rs_arrived(fr, c, nt)
            out_ref[fr, :, cols] += rbuf[fr, c, nt].astype(jnp.float32)

    def normalise(fr):
        values = norm(x_ref[fr].astype(jnp.float32), gain_ref[...]).astype(jnp.bfloat16)
        block(xg, fr, t)[...] = values

    def project(fr, b):
        at = pl.ds(pl.multiple_of(b * rows, rows), rows)
        tile = 256 if joined.shape[1] % 256 == 0 else joined.shape[1]
        for n in range(joined.shape[1] // tile):
            cols = pl.ds(n * tile, tile)
            weight = w_in[:, :, cols].reshape(width, tile)
            joined[:, cols] = jnp.dot(xg[fr, at, :], weight, preferred_element_type=jnp.float32)
        bf16 = jnp.bfloat16
        qkv[at, :head_dim] = norm(joined[:, :head_dim], qg_ref[...]).astype(bf16)
        qkv[at, head_dim:2 * head_dim] = norm(joined[:, head_dim:2 * head_dim], kg_ref[...]).astype(bf16)
        qkv[at, 2 * head_dim:] = joined[:, 2 * head_dim:3 * head_dim].astype(bf16)
        raw = joined[:, 3 * head_dim:]
        blended[at, head_dim:] = (0.5 * raw * (1.0 + lax.erf(raw * math.sqrt(0.5)))).astype(bf16)

    def project_step(fr, s):
        pl.when(t - 1 - s >= 0)(lambda: project(fr, t - 1 - s))
        pl.when(t + 1 + s < nt)(lambda: project(fr, t + 1 + s))

    def attend():
        query, key, value = (qkv[:, i * head_dim:(i + 1) * head_dim] for i in range(3))
        scores = lax.dot_general(query, key, (((1,), (1,)), ((), ())), preferred_element_type=jnp.float32)
        exp_scores = jnp.exp(scores * (1.0 / math.sqrt(head_dim)))
        total = jnp.sum(exp_scores, axis=-1, keepdims=True)
        attended = jnp.dot(exp_scores.astype(jnp.bfloat16), value, preferred_element_type=jnp.float32)
        blended[:, :head_dim] = (attended / total).astype(jnp.bfloat16)

    def contribute(fr, c):
        cols = w_out.shape[2]
        for n in range(nlo):
            part[fr, c, :, n * cols:(n + 1) * cols] = jnp.dot(
                blended[...], w_out[c * nlo + n], preferred_element_type=jnp.float32
            ).astype(jnp.bfloat16)

    for w in range(2):
        pltpu.make_async_copy(given[w], held[w].at[f], own_sem.at[w]).start()
    w_own_across(0, start)
    normalise(0)
    ag_own(0, start)
    w_own_sibling(0, start)
    w_own_across(1, start)
    for fr in range(1, frames):
        normalise(fr)
    w_own_sibling(1, start)

    def relays(step, w, lowest, highest):
        return [functools.partial(step, w, sub, start, True) for sub in range(lowest, min(highest, subs))]

    groups = [
        relays(w_relay, 0, 0, 1),
        relays(w_relay, 0, 1, subs) + relays(w_relay_two, 0, 0, 1) + relays(w_relay, 1, 0, 1),
        relays(w_relay_two, 0, 1, subs) + relays(w_relay, 1, 1, subs) + relays(w_relay_two, 1, 0, subs - 1),
    ]
    for k in range(nt - 2):
        for task in groups.pop(0) if groups else ():
            task()
        ag_tick(k, start, True)
    for task in sum(groups, []):
        task()
    for j in range(nhi):
        w_ready(0, j)
    project(0, t)
    pl.loop(0, nt - 2)(lambda s: project_step(0, s))
    ag_tick(nt - 2, start, True)
    project_step(0, nt - 2)
    attend()
    chunks = [lax.rem(hi + j, nhi) for j in range(nhi)]
    for fr in range(frames):
        for j, c in enumerate(chunks):
            if fr == 0:
                if j == min(1, nhi - 1):
                    for task in relays(w_relay_two, 1, subs - 1, subs):
                        task()
                w_ready(1, j)
            contribute(fr, c)
            rs_edge(fr, c)
        if fr + 1 < frames:
            project(fr + 1, t)
        if fr > 0:
            for c in chunks:
                rs_finish(fr - 1, c)

        @pl.loop(0, nt - 1)
        def _(s, fr=fr):
            if fr + 1 < frames:
                ag_tick((fr + 1) * (nt - 1) + s, start, True)
            for i in range(nhi):
                m = s * nhi + i
                rs_step(fr, lax.rem(hi + m // (nt - 1), nhi), m % (nt - 1))
            if fr + 1 < frames:
                project_step(fr + 1, s)

        if fr + 1 < frames:
            attend()
    for c in chunks:
        rs_finish(frames - 1, c)

    for w in range(2):
        w_sent(w)
    for fr in range(frames):
        for c in range(nhi):
            rs_sent(fr, c)
    ag_own(0, sent)
    for k in range(frames * (nt - 1)):
        ag_tick(k, sent, False)


def local(ng, nt, nf, patches, ln_gain, in_weight, q_gain, k_gain, out_weight):
    rows, frames, width = patches.shape
    depth, _, joined_cols = in_weight.shape
    _, out_rows, out_cols = out_weight.shape
    nlo = 2 if nf % 2 == 0 else 1
    nhi = nf // nlo
    subs = 2 if depth % (ng * 32) == 0 and out_rows % (ng * 32) == 0 else 1
    slots = max(nhi - 1, ng - 1) + 1
    everyone = nt * rows
    vmem = pl.BlockSpec(memory_space=pltpu.VMEM)
    hbm = pl.BlockSpec(memory_space=pl.ANY)
    bf16, f32 = jnp.bfloat16, jnp.float32
    dma = pltpu.SemaphoreType.DMA
    summed = pl.pallas_call(
        functools.partial(kernel, ng, nt, nf, nlo, subs),
        out_shape=jax.ShapeDtypeStruct((frames, rows, width), f32),
        in_specs=[vmem, vmem, hbm, vmem, vmem, hbm],
        out_specs=vmem,
        scratch_shapes=[
            pltpu.VMEM((frames, everyone, width), bf16),
            pltpu.VMEM((nf, depth, joined_cols), bf16),
            pltpu.VMEM((nf, out_rows, out_cols), bf16),
            pltpu.VMEM((rows, joined_cols), f32),
            pltpu.VMEM((everyone, 3 * q_gain.shape[1]), bf16),
            pltpu.VMEM((everyone, out_rows), bf16),
            pltpu.VMEM((frames, nhi, everyone, width // nhi), bf16),
            pltpu.VMEM((frames, nhi, nt + 1, rows, width // nhi), bf16),
            dma((frames, 2, nt)),
            dma((frames, nt)),
            dma((frames, nhi, nt)),
            dma((frames, nhi, nt + 1)),
            dma((2, nf, ng, subs, slots)),
            dma((2, nf, ng, subs)),
            dma((2,)),
        ],
        compiler_params=pltpu.CompilerParams(
            collective_id=0, has_side_effects=True, vmem_limit_bytes=48 * 1024 * 1024
        ),
    )(
        jnp.transpose(patches, (1, 0, 2)),
        ln_gain.reshape(1, width),
        in_weight.reshape(depth, joined_cols),
        q_gain,
        k_gain,
        out_weight.reshape(out_rows, out_cols),
    )
    return jnp.transpose(summed, (1, 0, 2)).astype(jnp.bfloat16)


def solution(mesh):
    sizes = [mesh.shape[name] for name in ("groups", "tensor", "frames")]
    return jax.shard_map(
        functools.partial(local, *sizes),
        mesh=mesh,
        in_specs=(
            P("tensor", ("groups", "frames"), None),
            P(),
            P("frames", "tensor", None),
            P("tensor", None),
            P("tensor", None),
            P("tensor", None, "frames"),
        ),
        out_specs=P("tensor", ("groups", "frames"), None),
        check_vma=False,
    )
```
